512 devices in a mesh: blk: 32 (over y, z_hi), team: 16 (over z_lo, x, core).
Axes of the slice: x: 4, y: 8, z: 8 (z_hi: 4, z_lo: 2; z = z_hi * 2 + z_lo), core: 2. Of those that a mesh axis runs over, the one named last changes fastest.
Arguments:
- points: bfloat16 [16, 65536], P(None, ('blk', 'team')), may hold values from -5 to 5
- inv_scale: float32 [16], replicated, may hold values from 0.5 to 1
- noise_var: float32 [65536], P(('blk', 'team')), may hold values from 0.2 to 2
- signal_var: float32 [1], replicated, may hold values from 0.5 to 2
- targets: float32 [32, 65536], P(None, ('blk', 'team')), may hold values from -6 to 6
Outputs:
- solution: float32 [32, 65536], P(None, ('blk', 'team'))
- residual: float32 [32, 65536], P(None, ('blk', 'team'))
The draws below stay inside these ranges and needn't reach their ends.
All inputs are finite; a program needn't handle non-finite values.
Results may differ from the reference program's by a relative error of at most 0.0048.
Values may be sent and summed in bfloat16 or wider, within the bound.
No kernel may reach another device: no remote copies, remote signals or barrier semaphores. Data moves between devices by JAX's collectives and lax.ppermute only.
A program may use at most 64 MiB of HBM per device.

```python
import math
import jax
import jax.numpy as jnp
from jax import lax

DIMS = 16
PROBES = 32
ITERS = 2
NPTS = 65536


def steps_of(rng, extent, split, low, largest):
    loudness, own = 1.0, jax.random.fold_in(rng, 6)
    for dim, parts in split:
        steps = jnp.exp(jax.random.uniform(jax.random.fold_in(own, dim), (parts,), jnp.float32, low / len(split), largest / len(split)))
        loudness = loudness * jnp.repeat(steps, extent[dim] // parts).reshape([-1 if axis == dim else 1 for axis in range(len(extent))])
    return loudness


def gaussian(stream_key, shape, scale, reach, shards=(), held_as=jnp.bfloat16):
    values = jax.random.normal(stream_key, shape, jnp.float32) * scale
    if len(shards) > 0:
        values = steps_of(stream_key, shape, shards, -0.22, 0.18) * values
    return jnp.clip(values, min=-reach, max=reach).astype(held_as)


def setup_inputs(seed: int = 0) -> dict:
    key_list = jax.random.split(jax.random.key(seed), 6)
    points = gaussian(key_list[0], (DIMS, NPTS), 1.0, 5.0, ((1, 512),))
    inv_scale = jnp.clip(jnp.exp(jax.random.uniform(key_list[1], (DIMS,), jnp.float32, math.log(0.5), math.log(1.0))), 0.5, 1.0)
    noise_var = jnp.clip(jnp.exp(math.log(2.0) - 2.3025851 * jax.random.uniform(key_list[2], (NPTS,), jnp.float32) ** steps_of(key_list[2], (NPTS,), ((0, 512),), -0.2, 0.2)), 0.2, 2.0)
    signal_var = jnp.clip(jnp.exp(jax.random.uniform(key_list[3], (1,), jnp.float32, math.log(0.5), math.log(2.0))), 0.5, 2.0)
    targets = gaussian(key_list[4], (PROBES, NPTS), 1.0, 6.0, ((1, 512),), jnp.float32)
    return dict(points=points, inv_scale=inv_scale, noise_var=noise_var, signal_var=signal_var, targets=targets)


def kernel_apply(scaled, sqnorm, lowered):
    block_rows = min(512, NPTS)
    blocks = NPTS // block_rows
    row_scaled = jnp.transpose(scaled.reshape(DIMS, blocks, block_rows), (1, 0, 2))
    row_norms = sqnorm.reshape(blocks, block_rows)

    def one_block(inputs):
        block_scaled, block_norms = inputs
        inner_prod = lax.dot_general(block_scaled, scaled, (((0,), (0,)), ((), ())), precision=lax.Precision.HIGHEST, preferred_element_type=jnp.float32)
        distance = block_norms[:, None] + sqnorm[None, :] - 2.0 * inner_prod
        kernel_tile = jnp.exp(-0.5 * distance).astype(jnp.bfloat16).astype(jnp.float32)
        return lax.dot_general(lowered, kernel_tile, (((1,), (1,)), ((), ())), precision=lax.Precision.HIGHEST, preferred_element_type=jnp.float32)

    result = lax.map(one_block, (row_scaled, row_norms))
    return jnp.transpose(result, (1, 0, 2)).reshape(PROBES, NPTS)


def reference(points, inv_scale, noise_var, signal_var, targets):
    scaled = points.astype(jnp.float32) * inv_scale[:, None]
    sqnorm = jnp.sum(scaled * scaled, axis=0)

    def apply_operator(vector):
        lowered = vector.astype(jnp.bfloat16).astype(jnp.float32)
        total = kernel_apply(scaled, sqnorm, lowered)
        return noise_var[None, :] * vector + signal_var[0] * total

    solution = jnp.zeros_like(targets)
    residual = targets
    direction = targets
    norm_now = jnp.sum(residual * residual, axis=1)
    for iteration in range(ITERS):
        applied = apply_operator(direction)
        step_size = norm_now / jnp.sum(direction * applied, axis=1)
        solution = solution + step_size[:, None] * direction
        residual = residual - step_size[:, None] * applied
        if iteration + 1 < ITERS:
            norm_next = jnp.sum(residual * residual, axis=1)
            direction = residual + (norm_next / norm_now)[:, None] * direction
            norm_now = norm_next
    return solution, residual
```

```python
import math

import jax
import jax.numpy as jnp
from jax import lax
from jax.experimental import pallas as pl
from jax.experimental.pallas import tpu as pltpu
from jax.sharding import PartitionSpec as P

f32, bf16 = jnp.float32, jnp.bfloat16
DIMS, PROBES, LANES = 16, 32, 128
FEATURES = 128
LOG2E = math.log2(math.e)
VMEM = pl.BlockSpec(memory_space=pltpu.VMEM)
PARAMS = pltpu.CompilerParams(vmem_limit_bytes=24 * 2**20)


def pieces(x):
    hi = x.astype(bf16).astype(f32)
    rest = x - hi
    mid = rest.astype(bf16).astype(f32)
    low = (rest - mid).astype(bf16).astype(f32)
    return hi, mid, low


def features(parts, halves):
    row = lax.broadcasted_iota(jnp.int32, (DIMS, LANES), 0)
    extra = jnp.zeros((DIMS, LANES), f32)
    for place, values in enumerate(halves):
        extra = jnp.where(row == place, jnp.broadcast_to(values, extra.shape), extra)
    blank = jnp.zeros((FEATURES - 4 * DIMS, LANES), f32)
    return jnp.concatenate([*parts, extra, blank], axis=0)


def half_norms(points, inv_scale):
    scaled = points * inv_scale
    return pieces((-0.5 * LOG2E) * jnp.sum(scaled * scaled, axis=0, keepdims=True))


def tile_kernel(inv_scale_ref, cols_ref, rows_ref, tile_ref, partial_ref, lhs, rhs, *, wide, deep):
    inv_scale = inv_scale_ref[...]
    n_cols, n_rows = cols_ref.shape[0], rows_ref.shape[0]
    one = jnp.ones((1, LANES), f32)

    def row_features(i, carry):
        points = rows_ref[i, :DIMS, :].astype(f32)
        weighted = points * (inv_scale * inv_scale * LOG2E)
        block = features(pieces(weighted), (one, one, one, *half_norms(points, inv_scale)))
        lhs[pl.ds(pl.multiple_of(i * LANES, LANES), LANES), :] = block.T.astype(bf16)
        return carry

    def col_features(i, carry):
        points = cols_ref[i].astype(f32)
        block = features((points, points, points), (*half_norms(points, inv_scale), one, one, one))
        rhs[:, pl.ds(pl.multiple_of(i * LANES, LANES), LANES)] = block.astype(bf16)
        return carry

    lax.fori_loop(0, n_rows, row_features, 0, unroll=4)
    lax.fori_loop(0, n_cols, col_features, 0, unroll=4)
    for c in range(0, n_cols * LANES, wide):

        def step(j, total):
            here = pl.ds(pl.multiple_of(j * deep, deep), deep)
            exponent = jnp.dot(lhs[here, :], rhs[:, c : c + wide], preferred_element_type=f32)
            block = jnp.exp2(exponent).astype(bf16)
            tile_ref[here, c : c + wide] = block
            v = jnp.concatenate([rows_ref[j * (deep // LANES) + m, DIMS:, :] for m in range(deep // LANES)], axis=1)
            return total + jnp.dot(v, block, preferred_element_type=f32)

        total = lax.fori_loop(0, n_rows * LANES // deep, step, jnp.zeros((PROBES, wide), f32))
        for m in range(wide // LANES):
            partial_ref[c // LANES + m] = total[:, m * LANES : (m + 1) * LANES]


def apply_kernel(tile_ref, v_ref, partial_ref, *, wide):
    v = jnp.concatenate([v_ref[m] for m in range(v_ref.shape[0])], axis=1)
    for c in range(0, tile_ref.shape[1], wide):
        total = jnp.dot(v, tile_ref[:, c : c + wide], preferred_element_type=f32)
        for m in range(wide // LANES):
            partial_ref[c // LANES + m] = total[:, m * LANES : (m + 1) * LANES]


def shards(points, inv_scale, noise_var, signal_var, targets):
    blks, teams = lax.axis_size("blk"), lax.axis_size("team")
    weight = signal_var[0]

    def to_all(x, axis, size):
        return lax.all_to_all(jnp.broadcast_to(x[None], (size, *x.shape)), axis, 0, 0)

    cols = to_all(points, "team", teams)
    rows = to_all(jnp.concatenate([points, targets.astype(bf16)], axis=0), "blk", blks)
    tile_shape = (blks * LANES, teams * LANES)
    tile, partial = pl.pallas_call(
        lambda *refs: tile_kernel(*refs, wide=1024, deep=1024),
        out_shape=(pltpu.VMEM(tile_shape, bf16), jax.ShapeDtypeStruct((teams, PROBES, LANES), f32)),
        in_specs=[VMEM] * 3,
        out_specs=[VMEM] * 2,
        scratch_shapes=[pltpu.VMEM((tile_shape[0], FEATURES), bf16), pltpu.VMEM((FEATURES, tile_shape[1]), bf16)],
        compiler_params=PARAMS,
        name="tile",
    )(jnp.broadcast_to(inv_scale[:, None], (DIMS, LANES)), cols, rows)

    def operator(field, partial):
        total = jnp.sum(lax.all_to_all(partial, "team", 0, 0), axis=0)
        return noise_var[None, :] * field + weight * total

    applied = operator(targets, partial)
    partial = pl.pallas_call(
        lambda *refs: apply_kernel(*refs, wide=512),
        out_shape=jax.ShapeDtypeStruct((teams, PROBES, LANES), f32),
        in_specs=[VMEM] * 2,
        out_specs=VMEM,
        compiler_params=PARAMS,
        name="apply",
    )(tile, to_all(applied.astype(bf16), "blk", blks))
    twice = operator(applied, partial)

    sums = jnp.stack(
        [
            jnp.sum(a * b, axis=1)
            for a, b in [
                (targets, targets),
                (targets, applied),
                (applied, applied),
                (targets, twice),
                (applied, twice),
            ]
        ]
    )
    sums = jnp.sum(to_all(sums, "team", teams), axis=0)
    sums = jnp.sum(to_all(sums, "blk", blks), axis=0)
    tt, ta, aa, tb, ab = [sums[i][:, None] for i in range(5)]
    step_0 = tt / ta
    norm_1 = tt - 2.0 * step_0 * ta + step_0 * step_0 * aa
    ratio = norm_1 / tt
    curvature = (1 + ratio) * (1 + ratio) * ta - (1 + ratio) * step_0 * (tb + aa) + step_0 * step_0 * ab
    step_1 = norm_1 / curvature
    residual = targets - step_0 * applied
    direction = residual + ratio * targets
    field = (1 + ratio) * applied - step_0 * twice
    return step_0 * targets + step_1 * direction, residual - step_1 * field


def solution(mesh):
    return jax.shard_map(
        shards,
        mesh=mesh,
        in_specs=(P(None, ("blk", "team")), P(), P(("blk", "team")), P(), P(None, ("blk", "team"))),
        out_specs=(P(None, ("blk", "team")), P(None, ("blk", "team"))),
        check_vma=False,
    )
```

```python
import math

import jax
import jax.numpy as jnp
from jax import lax
from jax.experimental import pallas as pl
from jax.experimental.pallas import tpu as pltpu
from jax.sharding import PartitionSpec as P

f32, bf16 = jnp.float32, jnp.bfloat16
DIMS, PROBES, LANES = 16, 32, 128
FEATURES = 128
LOG2E = math.log2(math.e)
VMEM = pl.BlockSpec(memory_space=pltpu.VMEM)
PARAMS = pltpu.CompilerParams(vmem_limit_bytes=24 * 2**20)


def pieces(x):
    hi = x.astype(bf16).astype(f32)
    rest = x - hi
    mid = rest.astype(bf16).astype(f32)
    low = (rest - mid).astype(bf16).astype(f32)
    return hi, mid, low


def features(parts, halves):
    row = lax.broadcasted_iota(jnp.int32, (DIMS, LANES), 0)
    extra = jnp.zeros((DIMS, LANES), f32)
    for place, values in enumerate(halves):
        extra = jnp.where(row == place, jnp.broadcast_to(values, extra.shape), extra)
    blank = jnp.zeros((FEATURES - 4 * DIMS, LANES), f32)
    return jnp.concatenate([*parts, extra, blank], axis=0)


def half_norms(points, inv_scale):
    scaled = points * inv_scale
    return pieces((-0.5 * LOG2E) * jnp.sum(scaled * scaled, axis=0, keepdims=True))


def tile_kernel(inv_scale_ref, cols_ref, rows_ref, tile_ref, partial_ref, lhs, rhs, *, wide, deep):
    inv_scale = inv_scale_ref[...]
    n_cols, n_rows = cols_ref.shape[0], rows_ref.shape[0]
    one = jnp.ones((1, LANES), f32)

    def row_features(i, carry):
        points = rows_ref[i, :DIMS, :].astype(f32)
        weighted = points * (inv_scale * inv_scale * LOG2E)
        block = features(pieces(weighted), (one, one, one, *half_norms(points, inv_scale)))
        lhs[pl.ds(pl.multiple_of(i * LANES, LANES), LANES), :] = block.T.astype(bf16)
        return carry

    def col_features(i, carry):
        points = cols_ref[i].astype(f32)
        block = features((points, points, points), (*half_norms(points, inv_scale), one, one, one))
        rhs[:, pl.ds(pl.multiple_of(i * LANES, LANES), LANES)] = block.astype(bf16)
        return carry

    lax.fori_loop(0, n_rows, row_features, 0, unroll=4)
    lax.fori_loop(0, n_cols, col_features, 0, unroll=4)
    for c in range(0, n_cols * LANES, wide):

        def step(j, total):
            here = pl.ds(pl.multiple_of(j * deep, deep), deep)
            exponent = jnp.dot(lhs[here, :], rhs[:, c : c + wide], preferred_element_type=f32)
            block = jnp.exp2(exponent).astype(bf16)
            tile_ref[here, c : c + wide] = block
            v = jnp.concatenate([rows_ref[j * (deep // LANES) + m, DIMS:, :] for m in range(deep // LANES)], axis=1)
            return total + jnp.dot(v, block, preferred_element_type=f32)

        total = lax.fori_loop(0, n_rows * LANES // deep, step, jnp.zeros((PROBES, wide), f32))
        for m in range(wide // LANES):
            partial_ref[c // LANES + m] = total[:, m * LANES : (m + 1) * LANES]


def apply_kernel(tile_ref, v_ref, partial_ref, *, wide):
    v = jnp.concatenate([v_ref[m] for m in range(v_ref.shape[0])], axis=1)
    for c in range(0, tile_ref.shape[1], wide):
        total = jnp.dot(v, tile_ref[:, c : c + wide], preferred_element_type=f32)
        for m in range(wide // LANES):
            partial_ref[c // LANES + m] = total[:, m * LANES : (m + 1) * LANES]


def shards(points, inv_scale, noise_var, signal_var, targets):
    blks, teams = lax.axis_size("blk"), lax.axis_size("team")
    weight = signal_var[0]

    def to_all(x, axis, size):
        return lax.all_to_all(jnp.broadcast_to(x[None], (size, *x.shape)), axis, 0, 0)

    points, inv_scale = lax.optimization_barrier(
        (points, jnp.broadcast_to(inv_scale[:, None], (DIMS, LANES)))
    )
    cols = to_all(points, "team", teams)
    rows = to_all(jnp.concatenate([points, targets.astype(bf16)], axis=0), "blk", blks)
    tile_shape = (blks * LANES, teams * LANES)
    tile, partial = pl.pallas_call(
        lambda *refs: tile_kernel(*refs, wide=1024, deep=1024),
        out_shape=(pltpu.VMEM(tile_shape, bf16), jax.ShapeDtypeStruct((teams, PROBES, LANES), f32)),
        in_specs=[VMEM] * 3,
        out_specs=[VMEM] * 2,
        scratch_shapes=[pltpu.VMEM((tile_shape[0], FEATURES), bf16), pltpu.VMEM((FEATURES, tile_shape[1]), bf16)],
        compiler_params=PARAMS,
        name="tile",
    )(inv_scale, cols, rows)

    def operator(field, partial):
        total = jnp.sum(lax.all_to_all(partial, "team", 0, 0), axis=0)
        return noise_var[None, :] * field + weight * total

    applied = operator(targets, partial)
    partial = pl.pallas_call(
        lambda *refs: apply_kernel(*refs, wide=512),
        out_shape=jax.ShapeDtypeStruct((teams, PROBES, LANES), f32),
        in_specs=[VMEM] * 2,
        out_specs=VMEM,
        compiler_params=PARAMS,
        name="apply",
    )(pltpu.with_memory_space_constraint(tile, pltpu.VMEM), to_all(applied.astype(bf16), "blk", blks))
    twice = operator(applied, partial)

    sums = jnp.stack(
        [
            jnp.sum(a * b, axis=1)
            for a, b in [
                (targets, targets),
                (targets, applied),
                (applied, applied),
                (targets, twice),
                (applied, twice),
            ]
        ]
    )
    sums = jnp.sum(to_all(sums, "team", teams), axis=0)
    sums = jnp.sum(to_all(sums, "blk", blks), axis=0)
    tt, ta, aa, tb, ab = [sums[i][:, None] for i in range(5)]
    step_0 = tt / ta
    norm_1 = tt - 2.0 * step_0 * ta + step_0 * step_0 * aa
    ratio = norm_1 / tt
    curvature = (1 + ratio) * (1 + ratio) * ta - (1 + ratio) * step_0 * (tb + aa) + step_0 * step_0 * ab
    step_1 = norm_1 / curvature
    residual = targets - step_0 * applied
    direction = residual + ratio * targets
    field = (1 + ratio) * applied - step_0 * twice
    return step_0 * targets + step_1 * direction, residual - step_1 * field


def solution(mesh):
    return jax.shard_map(
        shards,
        mesh=mesh,
        in_specs=(P(None, ("blk", "team")), P(), P(("blk", "team")), P(), P(None, ("blk", "team"))),
        out_specs=(P(None, ("blk", "team")), P(None, ("blk", "team"))),
        check_vma=False,
    )
```

```python
import math

import jax
import jax.numpy as jnp
from jax import lax
from jax.experimental import pallas as pl
from jax.experimental.pallas import tpu as pltpu
from jax.sharding import PartitionSpec as P

f32, bf16 = jnp.float32, jnp.bfloat16
DIMS, PROBES, LANES = 16, 32, 128
FEATURES = 128
EXTRA = 8
LOG2E = math.log2(math.e)
VMEM = pl.BlockSpec(memory_space=pltpu.VMEM)
HBM = pl.BlockSpec(memory_space=pltpu.HBM)
LARGE = pltpu.CompilerParams(vmem_limit_bytes=24 * 2**20)
SMALL = pltpu.CompilerParams(vmem_limit_bytes=8 * 2**20)


def pieces(x):
    hi = x.astype(bf16).astype(f32)
    rest = x - hi
    mid = rest.astype(bf16).astype(f32)
    low = (rest - mid).astype(bf16).astype(f32)
    return hi, mid, low


def features(parts, halves):
    row = lax.broadcasted_iota(jnp.int32, (DIMS, LANES), 0)
    extra = jnp.zeros((DIMS, LANES), f32)
    for place, values in enumerate(halves):
        extra = jnp.where(row == place, jnp.broadcast_to(values, extra.shape), extra)
    blank = jnp.zeros((FEATURES - 4 * DIMS, LANES), f32)
    return jnp.concatenate([*parts, extra, blank], axis=0)


def half_norms(points, inv_scale):
    scaled = points * inv_scale
    return pieces((-0.5 * LOG2E) * jnp.sum(scaled * scaled, axis=0, keepdims=True))


def tile_kernel(inv_scale_ref, cols_ref, rows_ref, tile_ref, partial_ref, lhs, rhs, held, sems, *, deep):
    inv_scale = inv_scale_ref[...]
    n_cols, n_rows = cols_ref.shape[0], rows_ref.shape[0]
    one = jnp.ones((1, LANES), f32)

    def row_features(i, carry):
        points = rows_ref[i, :DIMS, :].astype(f32)
        weighted = points * (inv_scale * inv_scale * LOG2E)
        block = features(pieces(weighted), (one, one, one, *half_norms(points, inv_scale)))
        lhs[pl.ds(pl.multiple_of(i * LANES, LANES), LANES), :] = block.T.astype(bf16)
        return carry

    def col_features(i, carry):
        points = cols_ref[i].astype(f32)
        block = features((points, points, points), (*half_norms(points, inv_scale), one, one, one))
        rhs[:, pl.ds(pl.multiple_of(i * LANES, LANES), LANES)] = block.astype(bf16)
        return carry

    lax.fori_loop(0, n_rows, row_features, 0, unroll=4)
    lax.fori_loop(0, n_cols, col_features, 0, unroll=4)

    def copy(j):
        here = pl.ds(pl.multiple_of(j * deep, deep), deep)
        return pltpu.make_async_copy(held.at[here, :], tile_ref.at[here, :], sems.at[j])

    chunks = n_rows * LANES // deep

    def step(j, total):
        here = pl.ds(pl.multiple_of(j * deep, deep), deep)
        exponent = jnp.dot(lhs[here, :], rhs[...], preferred_element_type=f32)
        block = jnp.exp2(exponent).astype(bf16)
        held[here, :] = block
        copy(j).start()
        v = jnp.concatenate([rows_ref[j * (deep // LANES) + m, DIMS:, :] for m in range(deep // LANES)], axis=1)
        return total + jnp.dot(v, block, preferred_element_type=f32)

    total = lax.fori_loop(0, chunks, step, jnp.zeros((PROBES, n_cols * LANES), f32))
    for m in range(n_cols):
        partial_ref[m] = total[:, m * LANES : (m + 1) * LANES]
    for j in range(chunks):
        copy(j).wait()


def apply_kernel(tile_ref, v_ref, partial_ref, held, sems, *, deep):
    chunks = tile_ref.shape[0] // deep

    def copy(j):
        here = pl.ds(pl.multiple_of(j * deep, deep), deep)
        return pltpu.make_async_copy(tile_ref.at[here, :], held.at[here, :], sems.at[j])

    for j in range(chunks):
        copy(j).start()

    def step(j, total):
        here = pl.ds(pl.multiple_of(j * deep, deep), deep)
        copy(j).wait()
        v = jnp.concatenate([v_ref[j * (deep // LANES) + m] for m in range(deep // LANES)], axis=1)
        return total + jnp.dot(v, held[here, :], preferred_element_type=f32)

    total = lax.fori_loop(0, chunks, step, jnp.zeros((PROBES, tile_ref.shape[1]), f32))
    for m in range(partial_ref.shape[0]):
        partial_ref[m] = total[:, m * LANES : (m + 1) * LANES]


def pack_kernel(weight_ref, partial_ref, cols_ref, targets_ref, applied_ref, noise_ref, message_ref):
    targets, applied = targets_ref[...], applied_ref[...]
    inner = jnp.zeros(targets.shape, f32)
    for m in range(partial_ref.shape[0]):
        message_ref[m, :PROBES, :] = partial_ref[m]
        inner = inner + cols_ref[m].astype(f32) * partial_ref[m]
    inner = weight_ref[0] * inner + noise_ref[...] * applied * applied
    lane = lax.broadcasted_iota(jnp.int32, (PROBES, LANES), 1)
    sums = jnp.zeros((PROBES, LANES), f32)
    for place, product in enumerate((targets * targets, targets * applied, applied * applied, inner)):
        sums = jnp.where(lane == place, jnp.sum(product, axis=1, keepdims=True), sums)
    sums = jnp.concatenate([sums, jnp.zeros((LANES - PROBES, LANES), f32)], axis=0).T[:EXTRA]
    for m in range(partial_ref.shape[0]):
        message_ref[m, PROBES:, :] = sums


def shards(points, inv_scale, noise_var, signal_var, targets):
    blks, teams = lax.axis_size("blk"), lax.axis_size("team")
    weight = signal_var[0]

    def to_all(x, axis, size):
        return lax.all_to_all(jnp.broadcast_to(x[None], (size, *x.shape)), axis, 0, 0)

    points, inv_scale = lax.optimization_barrier(
        (points, jnp.broadcast_to(inv_scale[:, None], (DIMS, LANES)))
    )
    cols = to_all(points, "team", teams)
    rows = to_all(jnp.concatenate([points, targets.astype(bf16)], axis=0), "blk", blks)
    tile_shape = (blks * LANES, teams * LANES)
    deep = 512
    sems = pltpu.SemaphoreType.DMA((tile_shape[0] // deep,))
    tile, partial = pl.pallas_call(
        lambda *refs: tile_kernel(*refs, deep=deep),
        out_shape=(pltpu.HBM(tile_shape, bf16), jax.ShapeDtypeStruct((teams, PROBES, LANES), f32)),
        in_specs=[VMEM] * 3,
        out_specs=[HBM, VMEM],
        scratch_shapes=[
            pltpu.VMEM((tile_shape[0], FEATURES), bf16),
            pltpu.VMEM((FEATURES, tile_shape[1]), bf16),
            pltpu.VMEM(tile_shape, bf16),
            sems,
        ],
        compiler_params=LARGE,
        name="tile",
    )(inv_scale, cols, rows)

    total = jnp.sum(lax.all_to_all(partial, "team", 0, 0), axis=0)
    applied = noise_var[None, :] * targets + weight * total
    lowered = applied.astype(bf16)
    partial = pl.pallas_call(
        lambda *refs: apply_kernel(*refs, deep=deep),
        out_shape=jax.ShapeDtypeStruct((teams, PROBES, LANES), f32),
        in_specs=[HBM, VMEM],
        out_specs=VMEM,
        scratch_shapes=[pltpu.VMEM(tile_shape, bf16), sems],
        compiler_params=LARGE,
        cost_estimate=pl.CostEstimate(
            flops=2 * PROBES * tile_shape[0] * tile_shape[1],
            bytes_accessed=2 * tile_shape[0] * tile_shape[1],
            transcendentals=0,
        ),
        name="apply",
    )(pltpu.with_memory_space_constraint(tile, pltpu.HBM), to_all(lowered, "blk", blks))
    message = pl.pallas_call(
        pack_kernel,
        out_shape=jax.ShapeDtypeStruct((teams, PROBES + EXTRA, LANES), f32),
        in_specs=[pl.BlockSpec(memory_space=pltpu.SMEM)] + [VMEM] * 5,
        out_specs=VMEM,
        compiler_params=SMALL,
        name="pack",
    )(signal_var, partial, to_all(lowered, "team", teams), targets, applied, noise_var[None, :])
    total = jnp.sum(lax.all_to_all(message, "team", 0, 0), axis=0)
    twice = noise_var[None, :] * applied + weight * total[:PROBES]

    sums = jnp.sum(to_all(total[PROBES:], "blk", blks), axis=0)
    tt, ta, aa, ab = [sums[i, :PROBES, None] for i in range(4)]
    step_0 = tt / ta
    norm_1 = tt - 2.0 * step_0 * ta + step_0 * step_0 * aa
    ratio = norm_1 / tt
    curvature = (1 + ratio) * (1 + ratio) * ta - 2.0 * (1 + ratio) * step_0 * aa + step_0 * step_0 * ab
    step_1 = norm_1 / curvature
    residual = targets - step_0 * applied
    direction = residual + ratio * targets
    field = (1 + ratio) * applied - step_0 * twice
    return step_0 * targets + step_1 * direction, residual - step_1 * field


def solution(mesh):
    return jax.shard_map(
        shards,
        mesh=mesh,
        in_specs=(P(None, ("blk", "team")), P(), P(("blk", "team")), P(), P(None, ("blk", "team"))),
        out_specs=(P(None, ("blk", "team")), P(None, ("blk", "team"))),
        check_vma=False,
    )
```

```python
import math

import jax
import jax.numpy as jnp
from jax import lax
from jax.experimental import pallas as pl
from jax.experimental.pallas import tpu as pltpu
from jax.sharding import PartitionSpec as P

f32, bf16 = jnp.float32, jnp.bfloat16
DIMS, PROBES, LANES = 16, 32, 128
FEATURES = 4 * DIMS
EXTRA = 8
LOG2E = math.log2(math.e)
VMEM = pl.BlockSpec(memory_space=pltpu.VMEM)
SMEM = pl.BlockSpec(memory_space=pltpu.SMEM)
HBM = pl.BlockSpec(memory_space=pltpu.HBM)
LARGE = pltpu.CompilerParams(vmem_limit_bytes=24 * 2**20)
SMALL = pltpu.CompilerParams(vmem_limit_bytes=8 * 2**20)


def pieces(x):
    hi = x.astype(bf16).astype(f32)
    rest = x - hi
    mid = rest.astype(bf16).astype(f32)
    low = (rest - mid).astype(bf16).astype(f32)
    return hi, mid, low


def features(parts, halves):
    row = lax.broadcasted_iota(jnp.int32, (DIMS, LANES), 0)
    extra = jnp.zeros((DIMS, LANES), f32)
    for place, values in enumerate(halves):
        extra = jnp.where(row == place, jnp.broadcast_to(values, extra.shape), extra)
    return jnp.concatenate([*parts, extra], axis=0)


def half_norms(points, inv_scale):
    scaled = points * inv_scale
    return pieces((-0.5 * LOG2E) * jnp.sum(scaled * scaled, axis=0, keepdims=True))


def tile_kernel(
    inv_scale_ref, cols_ref, rows_ref, field_ref, noise_ref,
    tile_ref, tail_ref, partial_ref, field_out_ref, noise_out_ref,
    lhs, rhs, held, sems, more_sems,
):
    copies = [
        pltpu.make_async_copy(field_ref, field_out_ref, more_sems.at[0]),
        pltpu.make_async_copy(noise_ref, noise_out_ref, more_sems.at[1]),
    ]
    for copy in copies:
        copy.start()
    inv_scale = inv_scale_ref[...]
    n_cols, n_rows = cols_ref.shape[0], rows_ref.shape[0]
    deep = tail_ref.shape[0]
    one = jnp.ones((1, LANES), f32)
    for i in range(n_cols):
        points = cols_ref[i].astype(f32)
        block = features((points, points, points), (*half_norms(points, inv_scale), one, one, one))
        rhs[:, i * LANES : (i + 1) * LANES] = block.astype(bf16)
    for i in range(n_rows):
        points = rows_ref[i, :DIMS, :].astype(f32)
        weighted = points * (inv_scale * inv_scale * LOG2E)
        block = features(pieces(weighted), (one, one, one, *half_norms(points, inv_scale)))
        lhs[i * LANES : (i + 1) * LANES, :] = block.T.astype(bf16)

    total = jnp.zeros((PROBES, n_cols * LANES), f32)
    for j, start in enumerate(range(0, n_rows * LANES, deep)):
        here = slice(start, start + deep)
        exponent = jnp.dot(lhs[here, :], rhs[...], preferred_element_type=f32)
        block = jnp.exp2(exponent).astype(bf16)
        if start + deep < n_rows * LANES:
            held[here, :] = block
            copies.append(pltpu.make_async_copy(held.at[here, :], tile_ref.at[here, :], sems.at[j]))
            copies[-1].start()
        else:
            tail_ref[...] = block
        v = jnp.concatenate([rows_ref[m, DIMS:, :] for m in range(start // LANES, (start + deep) // LANES)], axis=1)
        total = total + jnp.dot(v, block, preferred_element_type=f32)
    for m in range(n_cols):
        partial_ref[m] = total[:, m * LANES : (m + 1) * LANES]
    for copy in copies:
        copy.wait()


def combine_kernel(weight_ref, received_ref, field_ref, noise_ref, applied_ref, to_blk_ref, to_team_ref):
    total = received_ref[0]
    for m in range(1, received_ref.shape[0]):
        total = total + received_ref[m]
    applied = noise_ref[...] * field_ref[...] + weight_ref[0] * total
    applied_ref[...] = applied
    lowered = applied.astype(bf16)
    for copies_ref in (to_blk_ref, to_team_ref):
        for m in range(copies_ref.shape[0]):
            copies_ref[m] = lowered


def apply_kernel(tile_ref, tail_ref, v_ref, partial_ref, held, sems):
    deep, rows = tail_ref.shape[0], tile_ref.shape[0]

    def product(start, block):
        v = jnp.concatenate([v_ref[m] for m in range(start // LANES, (start + deep) // LANES)], axis=1)
        return jnp.dot(v, block, preferred_element_type=f32)

    copies = []
    for j, start in enumerate(range(0, rows, deep)):
        here = slice(start, start + deep)
        copies.append((start, pltpu.make_async_copy(tile_ref.at[here, :], held.at[here, :], sems.at[j])))
        copies[-1][1].start()
    total = product(rows, tail_ref[...])
    for start, copy in copies:
        copy.wait()
        total = total + product(start, held[start : start + deep, :])
    for m in range(partial_ref.shape[0]):
        partial_ref[m] = total[:, m * LANES : (m + 1) * LANES]


def pack_kernel(weight_ref, partial_ref, cols_ref, targets_ref, applied_ref, noise_ref, message_ref):
    targets, applied = targets_ref[...], applied_ref[...]
    inner = jnp.zeros(targets.shape, f32)
    for m in range(partial_ref.shape[0]):
        message_ref[m, :PROBES, :] = partial_ref[m]
        inner = inner + cols_ref[m].astype(f32) * partial_ref[m]
    inner = weight_ref[0] * inner + noise_ref[...] * applied * applied
    lane = lax.broadcasted_iota(jnp.int32, (PROBES, LANES), 1)
    sums = jnp.zeros((PROBES, LANES), f32)
    for place, product in enumerate((targets * targets, targets * applied, applied * applied, inner)):
        sums = jnp.where(lane == place, jnp.sum(product, axis=1, keepdims=True), sums)
    sums = jnp.concatenate([sums, jnp.zeros((LANES - PROBES, LANES), f32)], axis=0).T[:EXTRA]
    for m in range(partial_ref.shape[0]):
        message_ref[m, PROBES:, :] = sums


def in_hbm(x):
    return pltpu.with_memory_space_constraint(x, pltpu.HBM)


def shards(points, inv_scale, noise_var, signal_var, targets):
    blks, teams = lax.axis_size("blk"), lax.axis_size("team")

    def to_all(x, axis, size):
        return lax.all_to_all(jnp.broadcast_to(x[None], (size, *x.shape)), axis, 0, 0)

    cols = to_all(points, "team", teams)
    own = jnp.concatenate([points, targets.astype(bf16)], axis=0)
    own, inv_scale = lax.optimization_barrier((own, jnp.broadcast_to(inv_scale[:, None], (DIMS, LANES))))
    rows = to_all(own, "blk", blks)
    deep, wide = 512, teams * LANES
    tile_shape = (blks * LANES - deep, wide)
    sems = pltpu.SemaphoreType.DMA((tile_shape[0] // deep,))
    tile, tail, partial, field, noise = pl.pallas_call(
        tile_kernel,
        out_shape=(
            pltpu.HBM(tile_shape, bf16),
            jax.ShapeDtypeStruct((deep, wide), bf16),
            jax.ShapeDtypeStruct((teams, PROBES, LANES), f32),
            jax.ShapeDtypeStruct((PROBES, LANES), f32),
            jax.ShapeDtypeStruct((1, LANES), f32),
        ),
        in_specs=[VMEM] * 3 + [HBM] * 2,
        out_specs=[HBM] + [VMEM] * 4,
        scratch_shapes=[
            pltpu.VMEM((blks * LANES, FEATURES), bf16),
            pltpu.VMEM((FEATURES, wide), bf16),
            pltpu.VMEM(tile_shape, bf16),
            sems,
            pltpu.SemaphoreType.DMA((2,)),
        ],
        compiler_params=LARGE,
        name="tile",
    )(inv_scale, cols, rows, in_hbm(targets), in_hbm(noise_var[None, :]))

    applied, to_blk, to_team = pl.pallas_call(
        combine_kernel,
        out_shape=(
            jax.ShapeDtypeStruct((PROBES, LANES), f32),
            jax.ShapeDtypeStruct((blks, PROBES, LANES), bf16),
            jax.ShapeDtypeStruct((teams, PROBES, LANES), bf16),
        ),
        in_specs=[SMEM] + [VMEM] * 3,
        out_specs=[VMEM] * 3,
        compiler_params=SMALL,
        name="combine",
    )(signal_var, lax.all_to_all(partial, "team", 0, 0), field, noise)
    partial = pl.pallas_call(
        apply_kernel,
        out_shape=jax.ShapeDtypeStruct((teams, PROBES, LANES), f32),
        in_specs=[HBM, VMEM, VMEM],
        out_specs=VMEM,
        scratch_shapes=[pltpu.VMEM(tile_shape, bf16), sems],
        compiler_params=LARGE,
        cost_estimate=pl.CostEstimate(
            flops=2 * PROBES * tile_shape[0] * tile_shape[1],
            bytes_accessed=2 * tile_shape[0] * tile_shape[1],
            transcendentals=0,
        ),
        name="apply",
    )(in_hbm(tile), tail, lax.all_to_all(to_blk, "blk", 0, 0))
    message = pl.pallas_call(
        pack_kernel,
        out_shape=jax.ShapeDtypeStruct((teams, PROBES + EXTRA, LANES), f32),
        in_specs=[SMEM] + [VMEM] * 5,
        out_specs=VMEM,
        compiler_params=SMALL,
        name="pack",
    )(signal_var, partial, lax.all_to_all(to_team, "team", 0, 0), field, applied, noise)
    total = jnp.sum(lax.all_to_all(message, "team", 0, 0), axis=0)
    twice = noise * applied + signal_var[0] * total[:PROBES]

    sums = jnp.sum(to_all(total[PROBES:], "blk", blks), axis=0)
    tt, ta, aa, ab = [sums[i, :PROBES, None] for i in range(4)]
    step_0 = tt / ta
    norm_1 = tt - 2.0 * step_0 * ta + step_0 * step_0 * aa
    ratio = norm_1 / tt
    curvature = (1 + ratio) * (1 + ratio) * ta - 2.0 * (1 + ratio) * step_0 * aa + step_0 * step_0 * ab
    step_1 = norm_1 / curvature
    residual = field - step_0 * applied
    direction = residual + ratio * field
    slope = (1 + ratio) * applied - step_0 * twice
    return step_0 * field + step_1 * direction, residual - step_1 * slope


def solution(mesh):
    return jax.shard_map(
        shards,
        mesh=mesh,
        in_specs=(P(None, ("blk", "team")), P(), P(("blk", "team")), P(), P(None, ("blk", "team"))),
        out_specs=(P(None, ("blk", "team")), P(None, ("blk", "team"))),
        check_vma=False,
    )
```

```python
import math

import jax
import jax.numpy as jnp
from jax import lax
from jax.experimental import pallas as pl
from jax.experimental.pallas import tpu as pltpu
from jax.sharding import PartitionSpec as P

f32, bf16 = jnp.float32, jnp.bfloat16
DIMS, PROBES, LANES = 16, 32, 128
FEATURES = 4 * DIMS
EXTRA = 16
LOG2E = math.log2(math.e)
VMEM = pl.BlockSpec(memory_space=pltpu.VMEM)
HBM = pl.BlockSpec(memory_space=pltpu.HBM)
LARGE = pltpu.CompilerParams(vmem_limit_bytes=24 * 2**20)
SMALL = pltpu.CompilerParams(vmem_limit_bytes=8 * 2**20)


def pieces(x):
    hi = x.astype(bf16).astype(f32)
    rest = x - hi
    mid = rest.astype(bf16).astype(f32)
    low = (rest - mid).astype(bf16).astype(f32)
    return hi, mid, low


def features(parts, halves):
    row = lax.broadcasted_iota(jnp.int32, (DIMS, LANES), 0)
    extra = jnp.zeros((DIMS, LANES), f32)
    for place, values in enumerate(halves):
        extra = jnp.where(row == place, jnp.broadcast_to(values, extra.shape), extra)
    return jnp.concatenate([*parts, extra], axis=0)


def half_norms(points, inv_scale):
    scaled = points * inv_scale
    return pieces((-0.5 * LOG2E) * jnp.sum(scaled * scaled, axis=0, keepdims=True))


def tile_kernel(
    inv_scale_ref, cols_ref, rows_ref, field_ref, noise_ref,
    tile_ref, tail_ref, partial_ref, field_out_ref, noise_out_ref,
    lhs, rhs, held, sems, more_sems,
):
    copies = [
        pltpu.make_async_copy(field_ref, field_out_ref, more_sems.at[0]),
        pltpu.make_async_copy(noise_ref, noise_out_ref, more_sems.at[1]),
    ]
    for copy in copies:
        copy.start()
    inv_scale = inv_scale_ref[...]
    n_cols, n_rows = cols_ref.shape[0], rows_ref.shape[0]
    deep = tail_ref.shape[0]
    one = jnp.ones((1, LANES), f32)
    for i in range(n_cols):
        points = cols_ref[i].astype(f32)
        block = features((points, points, points), (*half_norms(points, inv_scale), one, one, one))
        rhs[:, i * LANES : (i + 1) * LANES] = block.astype(bf16)
    for i in range(n_rows):
        points = rows_ref[i, :DIMS, :].astype(f32)
        weighted = points * (inv_scale * inv_scale * LOG2E)
        block = features(pieces(weighted), (one, one, one, *half_norms(points, inv_scale)))
        lhs[i * LANES : (i + 1) * LANES, :] = block.T.astype(bf16)

    total = jnp.zeros((PROBES, n_cols * LANES), f32)
    for j, start in enumerate(range(0, n_rows * LANES, deep)):
        here = slice(start, start + deep)
        exponent = jnp.dot(lhs[here, :], rhs[...], preferred_element_type=f32)
        block = jnp.exp2(exponent).astype(bf16)
        if start + deep < n_rows * LANES:
            held[here, :] = block
            copies.append(pltpu.make_async_copy(held.at[here, :], tile_ref.at[here, :], sems.at[j]))
            copies[-1].start()
        else:
            tail_ref[...] = block
        v = jnp.concatenate([rows_ref[m, DIMS:, :] for m in range(start // LANES, (start + deep) // LANES)], axis=1)
        total = total + jnp.dot(v, block, preferred_element_type=f32)
    for m in range(n_cols):
        partial_ref[m] = total[:, m * LANES : (m + 1) * LANES]
    for copy in copies:
        copy.wait()


def combine_kernel(weight_ref, received_ref, field_ref, noise_ref, applied_ref, to_blk_ref, to_team_ref):
    total = received_ref[0]
    for m in range(1, received_ref.shape[0]):
        total = total + received_ref[m]
    applied = noise_ref[...] * field_ref[...] + weight_ref[...] * total
    applied_ref[...] = applied
    lowered = applied.astype(bf16)
    for copies_ref in (to_blk_ref, to_team_ref):
        for m in range(copies_ref.shape[0]):
            copies_ref[m] = lowered


def apply_kernel(tile_ref, tail_ref, v_ref, partial_ref, held, sems):
    deep, rows = tail_ref.shape[0], tile_ref.shape[0]

    def product(start, block):
        v = jnp.concatenate([v_ref[m] for m in range(start // LANES, (start + deep) // LANES)], axis=1)
        return jnp.dot(v, block, preferred_element_type=f32)

    copies = []
    for j, start in enumerate(range(0, rows, deep)):
        here = slice(start, start + deep)
        copies.append((start, pltpu.make_async_copy(tile_ref.at[here, :], held.at[here, :], sems.at[j])))
        copies[-1][1].start()
    total = product(rows, tail_ref[...])
    for start, copy in copies:
        copy.wait()
        total = total + product(start, held[start : start + deep, :])
    for m in range(partial_ref.shape[0]):
        partial_ref[m] = total[:, m * LANES : (m + 1) * LANES]


def pack_kernel(weight_ref, partial_ref, cols_ref, targets_ref, applied_ref, noise_ref, message_ref):
    targets, applied = targets_ref[...], applied_ref[...]
    inner = jnp.zeros(targets.shape, f32)
    for m in range(partial_ref.shape[0]):
        message_ref[m, :PROBES, :] = partial_ref[m].astype(bf16)
        inner = inner + cols_ref[m].astype(f32) * partial_ref[m]
    inner = weight_ref[...] * inner + noise_ref[...] * applied * applied
    lane = lax.broadcasted_iota(jnp.int32, (PROBES, LANES), 1)
    sums = jnp.zeros((PROBES, LANES), f32)
    for place, product in enumerate((targets * targets, targets * applied, applied * applied, inner)):
        for piece, part in enumerate(pieces(jnp.sum(product, axis=1, keepdims=True))):
            sums = jnp.where(lane == 4 * piece + place, part, sums)
    sums = jnp.concatenate([sums, jnp.zeros((LANES - PROBES, LANES), f32)], axis=0).T[:EXTRA].astype(bf16)
    for m in range(partial_ref.shape[0]):
        message_ref[m, PROBES:, :] = sums


def in_hbm(x):
    return pltpu.with_memory_space_constraint(x, pltpu.HBM)


def shards(points, inv_scale, noise_var, signal_var, targets):
    blks, teams = lax.axis_size("blk"), lax.axis_size("team")

    def to_all(x, axis, size):
        return lax.all_to_all(jnp.broadcast_to(x[None], (size, *x.shape)), axis, 0, 0)

    cols = to_all(points, "team", teams)
    own = jnp.concatenate([points, targets.astype(bf16)], axis=0)
    own, inv_scale, weight = lax.optimization_barrier(
        (own, jnp.broadcast_to(inv_scale[:, None], (DIMS, LANES)), jnp.broadcast_to(signal_var[None], (1, LANES)))
    )
    rows = to_all(own, "blk", blks)
    deep, wide = 512, teams * LANES
    tile_shape = (blks * LANES - deep, wide)
    sems = pltpu.SemaphoreType.DMA((tile_shape[0] // deep,))
    tile, tail, partial, field, noise = pl.pallas_call(
        tile_kernel,
        out_shape=(
            pltpu.HBM(tile_shape, bf16),
            jax.ShapeDtypeStruct((deep, wide), bf16),
            jax.ShapeDtypeStruct((teams, PROBES, LANES), f32),
            jax.ShapeDtypeStruct((PROBES, LANES), f32),
            jax.ShapeDtypeStruct((1, LANES), f32),
        ),
        in_specs=[VMEM] * 3 + [HBM] * 2,
        out_specs=[HBM] + [VMEM] * 4,
        scratch_shapes=[
            pltpu.VMEM((blks * LANES, FEATURES), bf16),
            pltpu.VMEM((FEATURES, wide), bf16),
            pltpu.VMEM(tile_shape, bf16),
            sems,
            pltpu.SemaphoreType.DMA((2,)),
        ],
        compiler_params=LARGE,
        name="tile",
    )(inv_scale, cols, rows, in_hbm(targets), in_hbm(noise_var[None, :]))

    applied, to_blk, to_team = pl.pallas_call(
        combine_kernel,
        out_shape=(
            jax.ShapeDtypeStruct((PROBES, LANES), f32),
            jax.ShapeDtypeStruct((blks, PROBES, LANES), bf16),
            jax.ShapeDtypeStruct((teams, PROBES, LANES), bf16),
        ),
        in_specs=[VMEM] + [VMEM] * 3,
        out_specs=[VMEM] * 3,
        compiler_params=SMALL,
        name="combine",
    )(weight, lax.all_to_all(partial, "team", 0, 0), field, noise)
    partial = pl.pallas_call(
        apply_kernel,
        out_shape=jax.ShapeDtypeStruct((teams, PROBES, LANES), f32),
        in_specs=[HBM, VMEM, VMEM],
        out_specs=VMEM,
        scratch_shapes=[pltpu.VMEM(tile_shape, bf16), sems],
        compiler_params=LARGE,
        cost_estimate=pl.CostEstimate(
            flops=2 * PROBES * tile_shape[0] * tile_shape[1],
            bytes_accessed=2 * tile_shape[0] * tile_shape[1],
            transcendentals=0,
        ),
        name="apply",
    )(in_hbm(tile), tail, lax.all_to_all(to_blk, "blk", 0, 0))
    message = pl.pallas_call(
        pack_kernel,
        out_shape=jax.ShapeDtypeStruct((teams, PROBES + EXTRA, LANES), bf16),
        in_specs=[VMEM] + [VMEM] * 5,
        out_specs=VMEM,
        compiler_params=SMALL,
        name="pack",
    )(weight, partial, lax.all_to_all(to_team, "team", 0, 0), field, applied, noise)
    total = jnp.sum(lax.all_to_all(message, "team", 0, 0).astype(f32), axis=0)
    twice = noise * applied + weight * total[:PROBES]

    sums = total[PROBES : PROBES + 8] + total[PROBES + 8 :]
    sums = jnp.sum(to_all(sums, "blk", blks), axis=0)
    tt, ta, aa, ab = [(sums[i] + sums[i + 4])[:PROBES, None] for i in range(4)]
    step_0 = tt / ta
    norm_1 = tt - 2.0 * step_0 * ta + step_0 * step_0 * aa
    ratio = norm_1 / tt
    curvature = (1 + ratio) * (1 + ratio) * ta - 2.0 * (1 + ratio) * step_0 * aa + step_0 * step_0 * ab
    step_1 = norm_1 / curvature
    residual = field - step_0 * applied
    direction = residual + ratio * field
    slope = (1 + ratio) * applied - step_0 * twice
    return step_0 * field + step_1 * direction, residual - step_1 * slope


def solution(mesh):
    return jax.shard_map(
        shards,
        mesh=mesh,
        in_specs=(P(None, ("blk", "team")), P(), P(("blk", "team")), P(), P(None, ("blk", "team"))),
        out_specs=(P(None, ("blk", "team")), P(None, ("blk", "team"))),
        check_vma=False,
    )
```

```python
import math

import jax
import jax.numpy as jnp
from jax import lax
from jax.experimental import pallas as pl
from jax.experimental.pallas import tpu as pltpu
from jax.sharding import PartitionSpec as P

f32, bf16 = jnp.float32, jnp.bfloat16
DIMS, PROBES, LANES = 16, 32, 128
FEATURES = 4 * DIMS
EXTRA = 16
LOG2E = math.log2(math.e)
VMEM = pl.BlockSpec(memory_space=pltpu.VMEM)
HBM = pl.BlockSpec(memory_space=pltpu.HBM)
LARGE = pltpu.CompilerParams(vmem_limit_bytes=24 * 2**20)
SMALL = pltpu.CompilerParams(vmem_limit_bytes=8 * 2**20)


def pieces(x):
    hi = x.astype(bf16).astype(f32)
    rest = x - hi
    mid = rest.astype(bf16).astype(f32)
    low = (rest - mid).astype(bf16).astype(f32)
    return hi, mid, low


def features(parts, halves):
    row = lax.broadcasted_iota(jnp.int32, (DIMS, LANES), 0)
    extra = jnp.zeros((DIMS, LANES), f32)
    for place, values in enumerate(halves):
        extra = jnp.where(row == place, jnp.broadcast_to(values, extra.shape), extra)
    return jnp.concatenate([*parts, extra], axis=0)


def half_norms(points, inv_scale):
    scaled = points * inv_scale
    return pieces((-0.5 * LOG2E) * jnp.sum(scaled * scaled, axis=0, keepdims=True))


def prepare_kernel(
    points_ref, inv_scale_ref, noise_ref, weight_ref, field_ref,
    to_team_ref, to_blk_ref, inv_scale_out_ref, noise_out_ref, weight_out_ref, field_out_ref,
    points, inv_scale, weight, sems,
):
    pairs = [
        (points_ref, points),
        (field_ref, field_out_ref),
        (inv_scale_ref, inv_scale),
        (weight_ref, weight),
        (noise_ref, noise_out_ref),
    ]
    copies = [pltpu.make_async_copy(source, target, sems.at[i]) for i, (source, target) in enumerate(pairs)]
    for copy in copies:
        copy.start()
    for copy in copies:
        copy.wait()
    own = points[...]
    for m in range(to_team_ref.shape[0]):
        to_team_ref[m] = own
    lowered = field_out_ref[...].astype(bf16)
    for m in range(to_blk_ref.shape[0]):
        to_blk_ref[m, :DIMS, :] = own
        to_blk_ref[m, DIMS:, :] = lowered
    row = lax.broadcasted_iota(jnp.int32, (DIMS, DIMS), 0)
    lane = lax.broadcasted_iota(jnp.int32, (DIMS, DIMS), 1)
    spread = jnp.where(row == lane, jnp.broadcast_to(inv_scale[...], (DIMS, DIMS)), 0.0)
    inv_scale_out_ref[...] = jnp.broadcast_to(jnp.sum(spread, axis=1, keepdims=True), (DIMS, LANES))
    weight_out_ref[...] = jnp.broadcast_to(weight[...], (1, LANES))


def tile_kernel(
    inv_scale_ref, cols_ref, rows_ref, tile_ref, tail_ref, partial_ref, lhs, rhs, held, sems
):
    copies = []
    inv_scale = inv_scale_ref[...]
    n_cols, n_rows = cols_ref.shape[0], rows_ref.shape[0]
    deep = tail_ref.shape[0]
    one = jnp.ones((1, LANES), f32)
    for i in range(n_cols):
        points = cols_ref[i].astype(f32)
        block = features((points, points, points), (*half_norms(points, inv_scale), one, one, one))
        rhs[:, i * LANES : (i + 1) * LANES] = block.astype(bf16)
    for i in range(n_rows):
        points = rows_ref[i, :DIMS, :].astype(f32)
        weighted = points * (inv_scale * inv_scale * LOG2E)
        block = features(pieces(weighted), (one, one, one, *half_norms(points, inv_scale)))
        lhs[i * LANES : (i + 1) * LANES, :] = block.T.astype(bf16)

    total = jnp.zeros((PROBES, n_cols * LANES), f32)
    for j, start in enumerate(range(0, n_rows * LANES, deep)):
        here = slice(start, start + deep)
        exponent = jnp.dot(lhs[here, :], rhs[...], preferred_element_type=f32)
        block = jnp.exp2(exponent).astype(bf16)
        if start + deep < n_rows * LANES:
            held[here, :] = block
            copies.append(pltpu.make_async_copy(held.at[here, :], tile_ref.at[here, :], sems.at[j]))
            copies[-1].start()
        else:
            tail_ref[...] = block
        v = jnp.concatenate([rows_ref[m, DIMS:, :] for m in range(start // LANES, (start + deep) // LANES)], axis=1)
        total = total + jnp.dot(v, block, preferred_element_type=f32)
    for m in range(n_cols):
        partial_ref[m] = total[:, m * LANES : (m + 1) * LANES]
    for copy in copies:
        copy.wait()


def combine_kernel(weight_ref, received_ref, field_ref, noise_ref, applied_ref, to_blk_ref, to_team_ref):
    total = received_ref[0]
    for m in range(1, received_ref.shape[0]):
        total = total + received_ref[m]
    applied = noise_ref[...] * field_ref[...] + weight_ref[...] * total
    applied_ref[...] = applied
    lowered = applied.astype(bf16)
    for copies_ref in (to_blk_ref, to_team_ref):
        for m in range(copies_ref.shape[0]):
            copies_ref[m] = lowered


def apply_kernel(tile_ref, tail_ref, v_ref, partial_ref, held, sems):
    deep, rows = tail_ref.shape[0], tile_ref.shape[0]

    def product(start, block):
        v = jnp.concatenate([v_ref[m] for m in range(start // LANES, (start + deep) // LANES)], axis=1)
        return jnp.dot(v, block, preferred_element_type=f32)

    copies = []
    for j, start in enumerate(range(0, rows, deep)):
        here = slice(start, start + deep)
        copies.append((start, pltpu.make_async_copy(tile_ref.at[here, :], held.at[here, :], sems.at[j])))
        copies[-1][1].start()
    total = product(rows, tail_ref[...])
    for start, copy in copies:
        copy.wait()
        total = total + product(start, held[start : start + deep, :])
    for m in range(partial_ref.shape[0]):
        partial_ref[m] = total[:, m * LANES : (m + 1) * LANES]


def pack_kernel(weight_ref, partial_ref, cols_ref, targets_ref, applied_ref, noise_ref, message_ref):
    targets, applied = targets_ref[...], applied_ref[...]
    inner = jnp.zeros(targets.shape, f32)
    for m in range(partial_ref.shape[0]):
        message_ref[m, :PROBES, :] = partial_ref[m].astype(bf16)
        inner = inner + cols_ref[m].astype(f32) * partial_ref[m]
    inner = weight_ref[...] * inner + noise_ref[...] * applied * applied
    lane = lax.broadcasted_iota(jnp.int32, (PROBES, LANES), 1)
    groups = []
    for product in (targets * targets, targets * applied, applied * applied, inner):
        group = jnp.zeros((PROBES, LANES), f32)
        for place, part in enumerate(pieces(jnp.sum(product, axis=1, keepdims=True))):
            group = jnp.where(lane == place, part, group)
        groups.append(group)
    sums = jnp.concatenate(groups, axis=0).T[:EXTRA].astype(bf16)
    for m in range(partial_ref.shape[0]):
        message_ref[m, PROBES:, :] = sums


def in_hbm(x):
    return pltpu.with_memory_space_constraint(x, pltpu.HBM)


def shards(points, inv_scale, noise_var, signal_var, targets):
    blks, teams = lax.axis_size("blk"), lax.axis_size("team")

    to_team, to_blk, inv_scale, noise, weight, field = pl.pallas_call(
        prepare_kernel,
        out_shape=(
            jax.ShapeDtypeStruct((teams, DIMS, LANES), bf16),
            jax.ShapeDtypeStruct((blks, DIMS + PROBES, LANES), bf16),
            jax.ShapeDtypeStruct((DIMS, LANES), f32),
            jax.ShapeDtypeStruct((1, LANES), f32),
            jax.ShapeDtypeStruct((1, LANES), f32),
            jax.ShapeDtypeStruct((PROBES, LANES), f32),
        ),
        in_specs=[pl.BlockSpec(memory_space=pl.ANY)] * 5,
        out_specs=[VMEM] * 6,
        scratch_shapes=[
            pltpu.VMEM((DIMS, LANES), bf16),
            pltpu.VMEM((1, DIMS), f32),
            pltpu.VMEM((1, 1), f32),
            pltpu.SemaphoreType.DMA((5,)),
        ],
        compiler_params=SMALL,
        name="prepare",
    )(in_hbm(points), in_hbm(inv_scale[None]), in_hbm(noise_var[None]), signal_var[None], in_hbm(targets))
    cols = lax.all_to_all(to_team, "team", 0, 0)
    rows = lax.all_to_all(to_blk, "blk", 0, 0)
    deep, wide = 512, teams * LANES
    tile_shape = (blks * LANES - deep, wide)
    sems = pltpu.SemaphoreType.DMA((tile_shape[0] // deep,))
    tile, tail, partial = pl.pallas_call(
        tile_kernel,
        out_shape=(
            pltpu.HBM(tile_shape, bf16),
            jax.ShapeDtypeStruct((deep, wide), bf16),
            jax.ShapeDtypeStruct((teams, PROBES, LANES), f32),
        ),
        in_specs=[VMEM] * 3,
        out_specs=[HBM] + [VMEM] * 2,
        scratch_shapes=[
            pltpu.VMEM((blks * LANES, FEATURES), bf16),
            pltpu.VMEM((FEATURES, wide), bf16),
            pltpu.VMEM(tile_shape, bf16),
            sems,
        ],
        compiler_params=LARGE,
        name="tile",
    )(inv_scale, cols, rows)

    applied, to_blk, to_team = pl.pallas_call(
        combine_kernel,
        out_shape=(
            jax.ShapeDtypeStruct((PROBES, LANES), f32),
            jax.ShapeDtypeStruct((blks, PROBES, LANES), bf16),
            jax.ShapeDtypeStruct((teams, PROBES, LANES), bf16),
        ),
        in_specs=[VMEM] + [VMEM] * 3,
        out_specs=[VMEM] * 3,
        compiler_params=SMALL,
        name="combine",
    )(weight, lax.all_to_all(partial, "team", 0, 0), field, noise)
    partial = pl.pallas_call(
        apply_kernel,
        out_shape=jax.ShapeDtypeStruct((teams, PROBES, LANES), f32),
        in_specs=[HBM, VMEM, VMEM],
        out_specs=VMEM,
        scratch_shapes=[pltpu.VMEM(tile_shape, bf16), sems],
        compiler_params=LARGE,
        cost_estimate=pl.CostEstimate(
            flops=2 * PROBES * tile_shape[0] * tile_shape[1],
            bytes_accessed=2 * tile_shape[0] * tile_shape[1],
            transcendentals=0,
        ),
        name="apply",
    )(in_hbm(tile), tail, lax.all_to_all(to_blk, "blk", 0, 0))
    message = pl.pallas_call(
        pack_kernel,
        out_shape=jax.ShapeDtypeStruct((teams, PROBES + EXTRA, LANES), bf16),
        in_specs=[VMEM] + [VMEM] * 5,
        out_specs=VMEM,
        compiler_params=SMALL,
        name="pack",
    )(weight, partial, lax.all_to_all(to_team, "team", 0, 0), field, applied, noise)
    total = jnp.sum(lax.all_to_all(message, "team", 0, 0).astype(f32), axis=0)
    twice = noise * applied + weight * total[:PROBES]

    sums = jnp.sum(total[PROBES:], axis=0, keepdims=True)
    sums = jnp.broadcast_to(sums[None], (blks, 1, LANES))
    sums = jnp.sum(lax.all_to_all(sums, "blk", 0, 0), axis=(0, 1))
    tt, ta, aa, ab = [sums[i * PROBES : (i + 1) * PROBES, None] for i in range(4)]
    step_0 = tt / ta
    norm_1 = tt - 2.0 * step_0 * ta + step_0 * step_0 * aa
    ratio = norm_1 / tt
    curvature = (1 + ratio) * (1 + ratio) * ta - 2.0 * (1 + ratio) * step_0 * aa + step_0 * step_0 * ab
    step_1 = norm_1 / curvature
    residual = field - step_0 * applied
    direction = residual + ratio * field
    slope = (1 + ratio) * applied - step_0 * twice
    return step_0 * field + step_1 * direction, residual - step_1 * slope


def solution(mesh):
    return jax.shard_map(
        shards,
        mesh=mesh,
        in_specs=(P(None, ("blk", "team")), P(), P(("blk", "team")), P(), P(None, ("blk", "team"))),
        out_specs=(P(None, ("blk", "team")), P(None, ("blk", "team"))),
        check_vma=False,
    )
```

```python
import math

import jax
import jax.numpy as jnp
from jax import lax
from jax.experimental import pallas as pl
from jax.experimental.pallas import tpu as pltpu
from jax.sharding import PartitionSpec as P

f32, bf16 = jnp.float32, jnp.bfloat16
DIMS, PROBES, LANES = 16, 32, 128
FEATURES = 4 * DIMS
EXTRA = 16
LOG2E = math.log2(math.e)
VMEM = pl.BlockSpec(memory_space=pltpu.VMEM)
HBM = pl.BlockSpec(memory_space=pltpu.HBM)
LARGE = pltpu.CompilerParams(vmem_limit_bytes=24 * 2**20)
SMALL = pltpu.CompilerParams(vmem_limit_bytes=8 * 2**20)


def pieces(x):
    hi = x.astype(bf16).astype(f32)
    rest = x - hi
    mid = rest.astype(bf16).astype(f32)
    low = (rest - mid).astype(bf16).astype(f32)
    return hi, mid, low


def features(parts, halves):
    row = lax.broadcasted_iota(jnp.int32, (DIMS, LANES), 0)
    extra = jnp.zeros((DIMS, LANES), f32)
    for place, values in enumerate(halves):
        extra = jnp.where(row == place, jnp.broadcast_to(values, extra.shape), extra)
    return jnp.concatenate([*parts, extra], axis=0)


def half_norms(points, inv_scale):
    scaled = points * inv_scale
    return pieces((-0.5 * LOG2E) * jnp.sum(scaled * scaled, axis=0, keepdims=True))


def prepare_kernel(
    points_ref, inv_scale_ref, noise_ref, weight_ref, field_ref,
    to_team_ref, to_blk_ref, inv_scale_out_ref, noise_out_ref, weight_out_ref, field_out_ref,
    points, inv_scale, weight, sems,
):
    pairs = [
        (points_ref, points),
        (field_ref, field_out_ref),
        (inv_scale_ref, inv_scale),
        (weight_ref, weight),
        (noise_ref, noise_out_ref),
    ]
    copies = [pltpu.make_async_copy(source, target, sems.at[i]) for i, (source, target) in enumerate(pairs)]
    for copy in copies:
        copy.start()
    for copy in copies:
        copy.wait()
    own = points[...]
    for m in range(to_team_ref.shape[0]):
        to_team_ref[m] = own
    lowered = field_out_ref[...].astype(bf16)
    for m in range(to_blk_ref.shape[0]):
        to_blk_ref[m, :DIMS, :] = own
        to_blk_ref[m, DIMS:, :] = lowered
    row = lax.broadcasted_iota(jnp.int32, (DIMS, DIMS), 0)
    lane = lax.broadcasted_iota(jnp.int32, (DIMS, DIMS), 1)
    spread = jnp.where(row == lane, jnp.broadcast_to(inv_scale[...], (DIMS, DIMS)), 0.0)
    inv_scale_out_ref[...] = jnp.broadcast_to(jnp.sum(spread, axis=1, keepdims=True), (DIMS, LANES))
    weight_out_ref[...] = jnp.broadcast_to(weight[...], (1, LANES))


def tile_kernel(
    inv_scale_ref, cols_ref, rows_ref, tile_ref, tail_ref, partial_ref, lhs, rhs, held, sems
):
    copies = []
    inv_scale = inv_scale_ref[...]
    n_cols, n_rows = cols_ref.shape[0], rows_ref.shape[0]
    deep = tail_ref.shape[0]
    one = jnp.ones((1, LANES), f32)
    for i in range(n_cols):
        points = cols_ref[i].astype(f32)
        block = features((points, points, points), (*half_norms(points, inv_scale), one, one, one))
        rhs[:, i * LANES : (i + 1) * LANES] = block.astype(bf16)
    for i in range(n_rows):
        points = rows_ref[i, :DIMS, :].astype(f32)
        weighted = points * (inv_scale * inv_scale * LOG2E)
        block = features(pieces(weighted), (one, one, one, *half_norms(points, inv_scale)))
        lhs[i * LANES : (i + 1) * LANES, :] = block.T.astype(bf16)

    total = jnp.zeros((PROBES, n_cols * LANES), f32)
    for j, start in enumerate(range(0, n_rows * LANES, deep)):
        here = slice(start, start + deep)
        exponent = jnp.dot(lhs[here, :], rhs[...], preferred_element_type=f32)
        block = jnp.exp2(exponent).astype(bf16)
        if start + deep < n_rows * LANES:
            held[here, :] = block
            copies.append(pltpu.make_async_copy(held.at[here, :], tile_ref.at[here, :], sems.at[j]))
            copies[-1].start()
        else:
            tail_ref[...] = block
        v = jnp.concatenate([rows_ref[m, DIMS:, :] for m in range(start // LANES, (start + deep) // LANES)], axis=1)
        total = total + jnp.dot(v, block, preferred_element_type=f32)
    for m in range(n_cols):
        partial_ref[m] = total[:, m * LANES : (m + 1) * LANES]
    for copy in copies:
        copy.wait()


def combine_kernel(weight_ref, received_ref, field_ref, noise_ref, applied_ref, to_blk_ref, to_team_ref):
    total = received_ref[0]
    for m in range(1, received_ref.shape[0]):
        total = total + received_ref[m]
    applied = noise_ref[...] * field_ref[...] + weight_ref[...] * total
    applied_ref[...] = applied
    lowered = applied.astype(bf16)
    for copies_ref in (to_blk_ref, to_team_ref):
        for m in range(copies_ref.shape[0]):
            copies_ref[m] = lowered


def apply_kernel(tile_ref, tail_ref, v_ref, partial_ref, held, sems):
    deep, rows = tail_ref.shape[0], tile_ref.shape[0]

    def product(start, block):
        v = jnp.concatenate([v_ref[m] for m in range(start // LANES, (start + deep) // LANES)], axis=1)
        return jnp.dot(v, block, preferred_element_type=f32)

    copies = []
    for j, start in enumerate(range(0, rows, deep)):
        here = slice(start, start + deep)
        copies.append((start, pltpu.make_async_copy(tile_ref.at[here, :], held.at[here, :], sems.at[j])))
        copies[-1][1].start()
    total = product(rows, tail_ref[...])
    for start, copy in copies:
        copy.wait()
        total = total + product(start, held[start : start + deep, :])
    for m in range(partial_ref.shape[0]):
        partial_ref[m] = total[:, m * LANES : (m + 1) * LANES]


def pack_kernel(weight_ref, partial_ref, cols_ref, targets_ref, applied_ref, noise_ref, message_ref, own_ref):
    here = lax.axis_index("team")
    targets, applied = targets_ref[...], applied_ref[...]
    inner = jnp.zeros(targets.shape, f32)
    for m in range(partial_ref.shape[0]):
        message_ref[m, :PROBES, :] = partial_ref[m].astype(bf16)
        inner = inner + cols_ref[m].astype(f32) * partial_ref[m]
    own_ref[...] = partial_ref[here]
    message_ref[here, :PROBES, :] = jnp.zeros((PROBES, LANES), bf16)
    inner = weight_ref[...] * inner + noise_ref[...] * applied * applied
    lane = lax.broadcasted_iota(jnp.int32, (PROBES, LANES), 1)
    groups = []
    for product in (targets * targets, targets * applied, applied * applied, inner):
        group = jnp.zeros((PROBES, LANES), f32)
        for place, part in enumerate(pieces(jnp.sum(product, axis=1, keepdims=True))):
            group = jnp.where(lane == place, part, group)
        groups.append(group)
    sums = jnp.concatenate(groups, axis=0).T[:EXTRA].astype(bf16)
    for m in range(partial_ref.shape[0]):
        message_ref[m, PROBES:, :] = sums


def rounded(x):
    return lax.reduce_precision(x, 8, 7)


def in_hbm(x):
    return pltpu.with_memory_space_constraint(x, pltpu.HBM)


def shards(points, inv_scale, noise_var, signal_var, targets):
    blks, teams = lax.axis_size("blk"), lax.axis_size("team")

    to_team, to_blk, inv_scale, noise, weight, field = pl.pallas_call(
        prepare_kernel,
        out_shape=(
            jax.ShapeDtypeStruct((teams, DIMS, LANES), bf16),
            jax.ShapeDtypeStruct((blks, DIMS + PROBES, LANES), bf16),
            jax.ShapeDtypeStruct((DIMS, LANES), f32),
            jax.ShapeDtypeStruct((1, LANES), f32),
            jax.ShapeDtypeStruct((1, LANES), f32),
            jax.ShapeDtypeStruct((PROBES, LANES), f32),
        ),
        in_specs=[pl.BlockSpec(memory_space=pl.ANY)] * 5,
        out_specs=[VMEM] * 6,
        scratch_shapes=[
            pltpu.VMEM((DIMS, LANES), bf16),
            pltpu.VMEM((1, DIMS), f32),
            pltpu.VMEM((1, 1), f32),
            pltpu.SemaphoreType.DMA((5,)),
        ],
        compiler_params=SMALL,
        name="prepare",
    )(in_hbm(points), in_hbm(inv_scale[None]), in_hbm(noise_var[None]), signal_var[None], in_hbm(targets))
    cols = lax.all_to_all(to_team, "team", 0, 0)
    rows = lax.all_to_all(to_blk, "blk", 0, 0)
    deep, wide = 512, teams * LANES
    tile_shape = (blks * LANES - deep, wide)
    sems = pltpu.SemaphoreType.DMA((tile_shape[0] // deep,))
    tile, tail, partial = pl.pallas_call(
        tile_kernel,
        out_shape=(
            pltpu.HBM(tile_shape, bf16),
            jax.ShapeDtypeStruct((deep, wide), bf16),
            jax.ShapeDtypeStruct((teams, PROBES, LANES), f32),
        ),
        in_specs=[VMEM] * 3,
        out_specs=[HBM] + [VMEM] * 2,
        scratch_shapes=[
            pltpu.VMEM((blks * LANES, FEATURES), bf16),
            pltpu.VMEM((FEATURES, wide), bf16),
            pltpu.VMEM(tile_shape, bf16),
            sems,
        ],
        compiler_params=LARGE,
        name="tile",
    )(inv_scale, cols, rows)

    applied, to_blk, to_team = pl.pallas_call(
        combine_kernel,
        out_shape=(
            jax.ShapeDtypeStruct((PROBES, LANES), f32),
            jax.ShapeDtypeStruct((blks, PROBES, LANES), bf16),
            jax.ShapeDtypeStruct((teams, PROBES, LANES), bf16),
        ),
        in_specs=[VMEM] * 4,
        out_specs=[VMEM] * 3,
        compiler_params=SMALL,
        name="combine",
    )(weight, lax.all_to_all(partial, "team", 0, 0), field, noise)
    partial = pl.pallas_call(
        apply_kernel,
        out_shape=jax.ShapeDtypeStruct((teams, PROBES, LANES), f32),
        in_specs=[HBM, VMEM, VMEM],
        out_specs=VMEM,
        scratch_shapes=[pltpu.VMEM(tile_shape, bf16), sems],
        compiler_params=LARGE,
        cost_estimate=pl.CostEstimate(
            flops=2 * PROBES * tile_shape[0] * tile_shape[1],
            bytes_accessed=2 * tile_shape[0] * tile_shape[1],
            transcendentals=0,
        ),
        name="apply",
    )(in_hbm(tile), tail, lax.all_to_all(to_blk, "blk", 0, 0))
    message, own = pl.pallas_call(
        pack_kernel,
        out_shape=(
            jax.ShapeDtypeStruct((teams, PROBES + EXTRA, LANES), bf16),
            jax.ShapeDtypeStruct((PROBES, LANES), f32),
        ),
        in_specs=[VMEM] * 6,
        out_specs=[VMEM] * 2,
        compiler_params=SMALL,
        name="pack",
    )(weight, partial, lax.all_to_all(to_team, "team", 0, 0), field, applied, noise)
    total = jnp.sum(lax.all_to_all(message, "team", 0, 0).astype(f32), axis=0)
    twice = noise * applied + weight * (total[:PROBES] + own)

    sums = jnp.sum(total[PROBES:], axis=0, keepdims=True)
    sums = jnp.broadcast_to(sums[None], (blks, 1, LANES))
    sums = jnp.sum(lax.all_to_all(sums, "blk", 0, 0), axis=(0, 1))
    tt, ta, aa, ab = [sums[i * PROBES : (i + 1) * PROBES, None] for i in range(4)]
    step_0 = tt / ta
    norm_1 = tt - 2.0 * step_0 * ta + step_0 * step_0 * aa
    ratio = norm_1 / tt
    curvature = (1 + ratio) * (1 + ratio) * ta - 2.0 * (1 + ratio) * step_0 * aa + step_0 * step_0 * ab
    step_1 = norm_1 / curvature
    residual = field - step_0 * applied
    direction = residual + ratio * field
    exact = (1 + ratio) * rounded(field) - step_0 * rounded(applied)
    slope = (1 + ratio) * applied - step_0 * twice + weight * (rounded(direction) - exact)
    return step_0 * field + step_1 * direction, residual - step_1 * slope


def solution(mesh):
    return jax.shard_map(
        shards,
        mesh=mesh,
        in_specs=(P(None, ("blk", "team")), P(), P(("blk", "team")), P(), P(None, ("blk", "team"))),
        out_specs=(P(None, ("blk", "team")), P(None, ("blk", "team"))),
        check_vma=False,
    )
```

```python
import math

import jax
import jax.numpy as jnp
from jax import lax
from jax.experimental import pallas as pl
from jax.experimental.pallas import tpu as pltpu
from jax.sharding import PartitionSpec as P

f32, bf16 = jnp.float32, jnp.bfloat16
DIMS, PROBES, LANES = 16, 32, 128
FEATURES = 4 * DIMS
EXTRA = 16
TINY = 1e-20
LOG2E = math.log2(math.e)
VMEM = pl.BlockSpec(memory_space=pltpu.VMEM)
HBM = pl.BlockSpec(memory_space=pltpu.HBM)
LARGE = pltpu.CompilerParams(vmem_limit_bytes=24 * 2**20)
SMALL = pltpu.CompilerParams(vmem_limit_bytes=8 * 2**20)


def pieces(x):
    hi = x.astype(bf16).astype(f32)
    rest = x - hi
    mid = rest.astype(bf16).astype(f32)
    low = (rest - mid).astype(bf16).astype(f32)
    return hi, mid, low


def features(parts, halves):
    row = lax.broadcasted_iota(jnp.int32, (DIMS, LANES), 0)
    extra = jnp.zeros((DIMS, LANES), f32)
    for place, values in enumerate(halves):
        extra = jnp.where(row == place, jnp.broadcast_to(values, extra.shape), extra)
    return jnp.concatenate([*parts, extra], axis=0)


def half_norms(points, inv_scale):
    scaled = points * inv_scale
    return pieces((-0.5 * LOG2E) * jnp.sum(scaled * scaled, axis=0, keepdims=True))


def prepare_kernel(
    points_ref, inv_scale_ref, noise_ref, weight_ref, field_ref,
    to_team_ref, to_blk_ref, inv_scale_out_ref, noise_out_ref, weight_out_ref, field_out_ref,
    points, inv_scale, weight, sems,
):
    pairs = [
        (points_ref, points),
        (field_ref, field_out_ref),
        (inv_scale_ref, inv_scale),
        (weight_ref, weight),
        (noise_ref, noise_out_ref),
    ]
    copies = [pltpu.make_async_copy(source, target, sems.at[i]) for i, (source, target) in enumerate(pairs)]
    for copy in copies:
        copy.start()
    for copy in copies:
        copy.wait()
    own = points[...]
    for m in range(to_team_ref.shape[0]):
        to_team_ref[m] = own
    lowered = field_out_ref[...].astype(bf16)
    for m in range(to_blk_ref.shape[0]):
        to_blk_ref[m, :DIMS, :] = own
        to_blk_ref[m, DIMS:, :] = lowered
    row = lax.broadcasted_iota(jnp.int32, (DIMS, DIMS), 0)
    lane = lax.broadcasted_iota(jnp.int32, (DIMS, DIMS), 1)
    spread = jnp.where(row == lane, jnp.broadcast_to(inv_scale[...], (DIMS, DIMS)), 0.0)
    inv_scale_out_ref[...] = jnp.broadcast_to(jnp.sum(spread, axis=1, keepdims=True), (DIMS, LANES))
    weight_out_ref[...] = jnp.broadcast_to(weight[...], (1, LANES))


def tile_kernel(
    inv_scale_ref, cols_ref, rows_ref, tile_ref, tail_ref, partial_ref, lhs, rhs, held, sems
):
    copies = []
    inv_scale = inv_scale_ref[...]
    n_cols, n_rows = cols_ref.shape[0], rows_ref.shape[0]
    deep = tail_ref.shape[0]
    one = jnp.ones((1, LANES), f32)
    for i in range(n_cols):
        points = cols_ref[i].astype(f32)
        block = features((points, points, points), (*half_norms(points, inv_scale), one, one, one))
        rhs[:, i * LANES : (i + 1) * LANES] = block.astype(bf16)
    for i in range(n_rows):
        points = rows_ref[i, :DIMS, :].astype(f32)
        weighted = points * (inv_scale * inv_scale * LOG2E)
        block = features(pieces(weighted), (one, one, one, *half_norms(points, inv_scale)))
        lhs[i * LANES : (i + 1) * LANES, :] = block.T.astype(bf16)

    total = jnp.zeros((PROBES, n_cols * LANES), f32)
    for j, start in enumerate(range(0, n_rows * LANES, deep)):
        here = slice(start, start + deep)
        exponent = jnp.dot(lhs[here, :], rhs[...], preferred_element_type=f32)
        block = jnp.exp2(exponent).astype(bf16)
        if start + deep < n_rows * LANES:
            held[here, :] = block
            copies.append(pltpu.make_async_copy(held.at[here, :], tile_ref.at[here, :], sems.at[j]))
            copies[-1].start()
        else:
            tail_ref[...] = block
        v = jnp.concatenate([rows_ref[m, DIMS:, :] for m in range(start // LANES, (start + deep) // LANES)], axis=1)
        total = total + jnp.dot(v, block, preferred_element_type=f32)
    for m in range(n_cols):
        partial_ref[m] = total[:, m * LANES : (m + 1) * LANES]
    for copy in copies:
        copy.wait()


def combine_kernel(
    weight_ref, received_ref, field_ref, noise_ref, product_ref, applied_ref, sent_ref, to_blk_ref, to_team_ref
):
    total = received_ref[0]
    for m in range(1, received_ref.shape[0]):
        total = total + received_ref[m]
    product_ref[...] = total
    field = field_ref[...]
    applied = noise_ref[...] * field + weight_ref[...] * total
    applied_ref[...] = applied
    ff, fa, aa = [jnp.sum(x, axis=1, keepdims=True) for x in (field * field, field * applied, applied * applied)]
    multiple = jnp.minimum(aa / jnp.maximum(fa, TINY), 4.0 * jnp.sqrt(aa / jnp.maximum(ff, TINY)))
    sent = applied - multiple * (field - field.astype(bf16).astype(f32))
    high = sent.astype(bf16)
    low = (sent - high.astype(f32)).astype(bf16)
    sent_ref[...] = high.astype(f32) + low.astype(f32)
    for copies_ref in (to_blk_ref, to_team_ref):
        for m in range(copies_ref.shape[0]):
            copies_ref[m, :PROBES, :] = high
            copies_ref[m, PROBES:, :] = low


def apply_kernel(tile_ref, tail_ref, v_ref, partial_ref, held, sems):
    deep, rows = tail_ref.shape[0], tile_ref.shape[0]

    def product(start, block):
        v = jnp.concatenate([v_ref[m] for m in range(start // LANES, (start + deep) // LANES)], axis=1)
        return jnp.dot(v, block, preferred_element_type=f32)

    copies = []
    for j, start in enumerate(range(0, rows, deep)):
        here = slice(start, start + deep)
        copies.append((start, pltpu.make_async_copy(tile_ref.at[here, :], held.at[here, :], sems.at[j])))
        copies[-1][1].start()
    total = product(rows, tail_ref[...])
    for start, copy in copies:
        copy.wait()
        total = total + product(start, held[start : start + deep, :])
    total = total[:PROBES] + total[PROBES:]
    for m in range(partial_ref.shape[0]):
        partial_ref[m] = total[:, m * LANES : (m + 1) * LANES]


def pack_kernel(
    weight_ref, partial_ref, cols_ref, field_ref, noise_ref, product_ref, applied_ref, sent_ref, message_ref, own_ref
):
    here = lax.axis_index("team")
    weight, noise = weight_ref[...], noise_ref[...]
    field, applied, product = field_ref[...], applied_ref[...], product_ref[...]
    inner = jnp.zeros(field.shape, f32)
    for m in range(partial_ref.shape[0]):
        message_ref[m, :PROBES, :] = partial_ref[m].astype(bf16)
        sent = cols_ref[m, :PROBES, :].astype(f32) + cols_ref[m, PROBES:, :].astype(f32)
        inner = inner + sent * partial_ref[m]
    own_ref[...] = partial_ref[here]
    message_ref[here, :PROBES, :] = jnp.zeros((PROBES, LANES), bf16)
    lane = lax.broadcasted_iota(jnp.int32, (PROBES, LANES), 1)

    def group(values, first):
        block = jnp.zeros((PROBES, LANES), f32)
        for place, part in enumerate(pieces(jnp.sum(values, axis=1, keepdims=True))):
            block = jnp.where(lane == first + place, part, block)
        return block

    lowered = field.astype(bf16).astype(f32)
    groups = [
        group(field * field, 0) + group(noise * field * applied + weight * sent_ref[...] * product, 8),
        group(field * applied, 0) + group(noise * applied * applied + weight * inner, 8),
        group(applied * applied, 0),
        group(noise * field * field + weight * lowered * product, 0),
    ]
    sums = jnp.concatenate(groups, axis=0).T[:EXTRA].astype(bf16)
    for m in range(partial_ref.shape[0]):
        message_ref[m, PROBES:, :] = sums


def rounded(x):
    return lax.reduce_precision(x, 8, 7)


def in_hbm(x):
    return pltpu.with_memory_space_constraint(x, pltpu.HBM)


def shards(points, inv_scale, noise_var, signal_var, targets):
    blks, teams = lax.axis_size("blk"), lax.axis_size("team")

    to_team, to_blk, inv_scale, noise, weight, field = pl.pallas_call(
        prepare_kernel,
        out_shape=(
            jax.ShapeDtypeStruct((teams, DIMS, LANES), bf16),
            jax.ShapeDtypeStruct((blks, DIMS + PROBES, LANES), bf16),
            jax.ShapeDtypeStruct((DIMS, LANES), f32),
            jax.ShapeDtypeStruct((1, LANES), f32),
            jax.ShapeDtypeStruct((1, LANES), f32),
            jax.ShapeDtypeStruct((PROBES, LANES), f32),
        ),
        in_specs=[pl.BlockSpec(memory_space=pl.ANY)] * 5,
        out_specs=[VMEM] * 6,
        scratch_shapes=[
            pltpu.VMEM((DIMS, LANES), bf16),
            pltpu.VMEM((1, DIMS), f32),
            pltpu.VMEM((1, 1), f32),
            pltpu.SemaphoreType.DMA((5,)),
        ],
        compiler_params=SMALL,
        name="prepare",
    )(in_hbm(points), in_hbm(inv_scale[None]), in_hbm(noise_var[None]), signal_var[None], in_hbm(targets))
    cols = lax.all_to_all(to_team, "team", 0, 0)
    rows = lax.all_to_all(to_blk, "blk", 0, 0)
    deep, wide = 512, teams * LANES
    tile_shape = (blks * LANES - deep, wide)
    sems = pltpu.SemaphoreType.DMA((tile_shape[0] // deep,))
    tile, tail, partial = pl.pallas_call(
        tile_kernel,
        out_shape=(
            pltpu.HBM(tile_shape, bf16),
            jax.ShapeDtypeStruct((deep, wide), bf16),
            jax.ShapeDtypeStruct((teams, PROBES, LANES), f32),
        ),
        in_specs=[VMEM] * 3,
        out_specs=[HBM] + [VMEM] * 2,
        scratch_shapes=[
            pltpu.VMEM((blks * LANES, FEATURES), bf16),
            pltpu.VMEM((FEATURES, wide), bf16),
            pltpu.VMEM(tile_shape, bf16),
            sems,
        ],
        compiler_params=LARGE,
        name="tile",
    )(inv_scale, cols, rows)

    block = jax.ShapeDtypeStruct((PROBES, LANES), f32)
    product, applied, sent, to_blk, to_team = pl.pallas_call(
        combine_kernel,
        out_shape=(
            block,
            block,
            block,
            jax.ShapeDtypeStruct((blks, 2 * PROBES, LANES), bf16),
            jax.ShapeDtypeStruct((teams, 2 * PROBES, LANES), bf16),
        ),
        in_specs=[VMEM] * 4,
        out_specs=[VMEM] * 5,
        compiler_params=SMALL,
        name="combine",
    )(weight, lax.all_to_all(partial, "team", 0, 0), field, noise)
    partial = pl.pallas_call(
        apply_kernel,
        out_shape=jax.ShapeDtypeStruct((teams, PROBES, LANES), f32),
        in_specs=[HBM, VMEM, VMEM],
        out_specs=VMEM,
        scratch_shapes=[pltpu.VMEM(tile_shape, bf16), sems],
        compiler_params=LARGE,
        cost_estimate=pl.CostEstimate(
            flops=2 * PROBES * tile_shape[0] * tile_shape[1],
            bytes_accessed=2 * tile_shape[0] * tile_shape[1],
            transcendentals=0,
        ),
        name="apply",
    )(in_hbm(tile), tail, lax.all_to_all(to_blk, "blk", 0, 0))
    message, own = pl.pallas_call(
        pack_kernel,
        out_shape=(
            jax.ShapeDtypeStruct((teams, PROBES + EXTRA, LANES), bf16),
            block,
        ),
        in_specs=[VMEM] * 8,
        out_specs=[VMEM] * 2,
        compiler_params=SMALL,
        name="pack",
    )(weight, partial, lax.all_to_all(to_team, "team", 0, 0), field, noise, product, applied, sent)
    total = jnp.sum(lax.all_to_all(message, "team", 0, 0).astype(f32), axis=0)
    twice = noise * applied + weight * (total[:PROBES] + own)

    sums = jnp.sum(total[PROBES:].reshape(2, EXTRA // 2, LANES), axis=1)
    sums = jnp.broadcast_to(sums[None], (blks, 2, LANES))
    sums = jnp.sum(lax.all_to_all(sums, "blk", 0, 0), axis=0)
    tt, ta, aa, c0 = [sums[0, i * PROBES : (i + 1) * PROBES, None] for i in range(4)]
    c1, c2 = [sums[1, i * PROBES : (i + 1) * PROBES, None] for i in range(2)]
    step_0 = tt / ta
    norm_1 = tt - 2.0 * step_0 * ta + step_0 * step_0 * aa
    ratio = norm_1 / tt
    curvature = (1 + ratio) * (1 + ratio) * c0 - 2.0 * (1 + ratio) * step_0 * c1 + step_0 * step_0 * c2
    step_1 = norm_1 / curvature
    residual = field - step_0 * applied
    direction = residual + ratio * field
    exact = (1 + ratio) * rounded(field) - step_0 * sent
    slope = (1 + ratio) * applied - step_0 * twice + weight * (rounded(direction) - exact)
    return step_0 * field + step_1 * direction, residual - step_1 * slope


def solution(mesh):
    return jax.shard_map(
        shards,
        mesh=mesh,
        in_specs=(P(None, ("blk", "team")), P(), P(("blk", "team")), P(), P(None, ("blk", "team"))),
        out_specs=(P(None, ("blk", "team")), P(None, ("blk", "team"))),
        check_vma=False,
    )
```
